32 devices in a mesh: tower: 2 (over core), batch: 16 (over z, y, x).
Axes of the slice: x: 2, y: 2, z: 4, core: 2. Of those that a mesh axis runs over, the one named last changes fastest.
Arguments:
- tokens: bfloat16 [2, 16, 512, 768], P('tower', 'batch'), may hold values from -6 to 6
- segments: int32 [2, 16, 512], P('tower', 'batch'), may hold values from 0 to 8, as said below
- w_query: bfloat16 [768, 768], replicated, may hold values from -0.02734375 to 0.02734375
- w_key: bfloat16 [768, 768], replicated, may hold values from -0.21875 to 0.21875
- w_value: bfloat16 [768, 768], replicated, may hold values from -0.21875 to 0.21875
- w_output: bfloat16 [768, 768], replicated, may hold values from -0.875 to 0.875
- w_gate: bfloat16 [768, 3072], replicated, may hold values from -0.21875 to 0.21875
- w_up: bfloat16 [768, 3072], replicated, may hold values from -0.21875 to 0.21875
- w_down: bfloat16 [3072, 768], replicated, may hold values from -0.15625 to 0.15625
- gain_attn: float32 [768], replicated, may hold values from 0.25 to 1.75
- gain_ffn: float32 [768], replicated, may hold values from 0.25 to 1.75
- gain_final: float32 [768], replicated, may hold values from 0.25 to 1.75
- bias_table: float32 [32, 12], replicated, may hold values from -4 to 4
- out_grad: bfloat16 [2, 16, 512, 768], P('tower', 'batch'), may hold values from -6 to 6
- score_grad: float32 [128, 128], P('batch'), may hold values from -6 to 6
Outputs:
- output: bfloat16 [2, 16, 512, 768], P('tower', 'batch')
- scores: float32 [128, 128], P('batch')
- grad_tokens: bfloat16 [2, 16, 512, 768], P('tower', 'batch')
- grad_w_query: float32 [768, 768], P(None, 'batch')
- grad_w_key: float32 [768, 768], P(None, 'batch')
- grad_w_value: float32 [768, 768], P(None, 'batch')
- grad_w_output: float32 [768, 768], P(None, 'batch')
- grad_w_gate: float32 [768, 3072], P(None, 'batch')
- grad_w_up: float32 [768, 3072], P(None, 'batch')
- grad_w_down: float32 [3072, 768], P(None, 'batch')
- grad_gain_attn: float32 [768], P('batch')
- grad_gain_ffn: float32 [768], P('batch')
- grad_gain_final: float32 [768], P('batch')
- grad_bias_table: float32 [32, 12], replicated
The draws below stay inside these ranges and needn't reach their ends.
Inputs may be any that keep to these rules, and one draw needn't show every extreme that they name: `segments`: each row of 512 tokens holds the items 1 to 8 in this order, each a run of one or more tokens, followed by one or more padding tokens of id 0.
All inputs are finite; a program needn't handle non-finite values.
Results may differ from the reference program's by a relative error of at most 0.015.
Values may be sent and summed in bfloat16 or wider, within the bound.
No kernel may reach another device: no remote copies, remote signals or barrier semaphores. Data moves between devices by JAX's collectives and lax.ppermute only.
A program may use at most 256 MiB of HBM per device.

```python
import math
import jax
import jax.numpy as jnp
import numpy as np
from jax import lax

D = 768
H = 12
DK = 64
FF = 3072
BUCKETS = 32
L = 512
ITEMS = 8
ROWS = 16
NI = 128


def draw_segments(key, part):
    key = jax.random.fold_in(key, 11)
    random_scores = jax.random.randint(key, (2, ROWS, L - 1), 0, 1 << 20, dtype=jnp.int32)
    ranked = random_scores * L + jnp.arange(L - 1, dtype=jnp.int32)
    picked = lax.top_k(ranked, ITEMS)[1].astype(jnp.int32) + 1
    places = jnp.arange(L, dtype=jnp.int32)
    passed = jnp.sum((picked[:, :, None, :] <= places[None, None, :, None]).astype(jnp.int32), axis=-1)
    return jnp.where(passed < ITEMS, passed + 1, 0).astype(jnp.int32)


def raised(array, rng, source, target, parts, factor):
    def block_of(axis_at):
        return (jnp.arange(array.shape[axis_at]) // (array.shape[axis_at] // parts)).reshape((-1,) + (1,) * (array.ndim - 1 - axis_at))

    first = jax.random.permutation(rng, parts)[block_of(target)]
    far = (block_of(target) + parts // 2) % parts
    return jnp.where((block_of(source) == first) | (block_of(source) == far), factor * array, array)


def levels(stream_key, extent, cuts, smallest, high):
    gain, own = 1.0, jax.random.fold_in(stream_key, 6)
    for axis_at, parts in cuts:
        heights = jnp.exp(jax.random.uniform(jax.random.fold_in(own, axis_at), (parts,), jnp.float32, smallest / len(cuts), high / len(cuts)))
        gain = gain * jnp.repeat(heights, extent[axis_at] // parts).reshape([-1 if axis == axis_at else 1 for axis in range(len(extent))])
    return gain


def scatter_about(rng, shape, width, reach, shards=(), kind=jnp.bfloat16):
    gain = levels(rng, shape, shards, -0.22, 0.18) if shards else 1.0
    entries = jax.random.normal(rng, shape, jnp.float32) * width * gain
    return jnp.minimum(jnp.maximum(entries, -reach), reach).astype(kind)


def bell_draw_with(key, dims, deviation, limit, shards, heavy, kind=jnp.bfloat16):
    array = deviation * jax.random.normal(key, dims, jnp.float32)
    if shards:
        array = array * levels(key, dims, shards, -0.22, 0.18)
    return jnp.clip(raised(array, jax.random.fold_in(key, 3), *heavy), -limit, limit).astype(kind)


def setup_inputs(seed: int = 0) -> dict:
    streams_of = jax.random.split(jax.random.key(seed), 16)
    return {
        "tokens": scatter_about(streams_of[0], (2, ROWS, L, D), 1.0, 6.0, ((0, 2), (1, 16))),
        "segments": draw_segments(jax.random.fold_in(streams_of[15], 71), 0),
        "w_query": scatter_about(streams_of[2], (D, D), (D * DK) ** -0.5, 0.02734375),
        "w_key": scatter_about(streams_of[3], (D, D), D ** -0.5, 0.21875),
        "w_value": scatter_about(streams_of[4], (D, D), D ** -0.5, 0.21875),
        "w_output": scatter_about(streams_of[5], (D, D), (D // 16) ** -0.5, 0.875),
        "w_gate": scatter_about(streams_of[6], (D, FF), D ** -0.5, 0.21875),
        "w_up": scatter_about(streams_of[7], (D, FF), D ** -0.5, 0.21875),
        "w_down": scatter_about(streams_of[8], (FF, D), (FF // 2) ** -0.5, 0.15625),
        "gain_attn": jnp.clip(1.0 + 0.15 * jax.random.normal(streams_of[9], (D,), jnp.float32), 0.25, 1.75),
        "gain_ffn": jnp.clip(1.0 + 0.15 * jax.random.normal(streams_of[10], (D,), jnp.float32), 0.25, 1.75),
        "gain_final": jnp.clip(1.0 + 0.15 * jax.random.normal(streams_of[11], (D,), jnp.float32), 0.25, 1.75),
        "bias_table": scatter_about(streams_of[12], (BUCKETS, H), 1.0, 4.0, (), jnp.float32),
        "out_grad": scatter_about(streams_of[13], (2, ROWS, L, D), 1.0, 6.0, ((0, 2), (1, 16))),
        "score_grad": bell_draw_with(streams_of[14], (NI, NI), 1.0, 6.0, ((0, 16),), (0, 1, 16, 2.0), jnp.float32),
    }


@jax.custom_vjp
def low(v):
    return lax.optimization_barrier(v.astype(jnp.bfloat16)).astype(jnp.float32)

@jax.custom_vjp
def low_back(v):
    return v

def low_keep(v):
    return (low(v), None)

def low_pass(kept, grad):
    return (grad,)

def back_keep(v):
    return (v, None)

def back_low(kept, grad):
    return (low(grad),)
low.defvjp(low_keep, low_pass)
low_back.defvjp(back_keep, back_low)
eps_norm = 1e-06
temper = 0.05
max_distance = 128
highest = lax.Precision.HIGHEST
masked_value = -1000000000.0

def bucket_table(length, bucket_count):
    relative = np.arange(length)[None, :] - np.arange(length)[:, None]
    halfway = bucket_count // 2
    upper_part = np.where(relative > 0, halfway, 0)
    distance = np.abs(relative)
    exact_span = halfway // 2
    scaled = np.log(np.maximum(distance, 1) / exact_span) / np.log(max_distance / exact_span) * (halfway - exact_span)
    far_bucket = np.minimum(exact_span + np.floor(np.maximum(scaled, 0.0)).astype(np.int32), halfway - 1)
    return (upper_part + np.where(distance < exact_span, distance, far_bucket)).astype(np.int32)

def rms_scale(values):
    return lax.rsqrt(lax.optimization_barrier(jnp.mean(values * values, axis=-1, keepdims=True)) + eps_norm)

def both_ways(values):
    return low(low_back(values))

def block_layer(params, inputs, segment):
    w_query, w_key, w_value, w_output, w_gate, w_up, w_down, gain_attn, gain_ffn, gain_final, bias_table = params
    rows_here, length, model_width = inputs.shape
    head_count = bias_table.shape[1]
    head_size = model_width // head_count
    row_shape = (rows_here, length, head_count, head_size)
    bucket_ids = bucket_table(length, bias_table.shape[0])
    bias_full = jnp.transpose(bias_table[bucket_ids], (2, 0, 1))
    normed = low(inputs * rms_scale(inputs) * gain_attn)
    query_proj = both_ways(jnp.einsum('rld,de->rle', normed, w_query, precision=highest)).reshape(row_shape)
    key_proj = both_ways(jnp.einsum('rld,de->rle', normed, w_key, precision=highest)).reshape(row_shape)
    value_proj = both_ways(jnp.einsum('rld,de->rle', normed, w_value, precision=highest)).reshape(row_shape)
    logits = jnp.einsum('rihd,rjhd->rhij', query_proj, key_proj, precision=highest) + bias_full[None]
    same_item = (segment[:, :, None] == segment[:, None, :])[:, None]
    logits = low_back(jnp.where(same_item, logits, masked_value))
    attn_probs = low(jax.nn.softmax(logits, axis=-1))
    mixed = jnp.einsum('rhij,rjhd->rihd', attn_probs, value_proj, precision=highest)
    mixed = both_ways(mixed.reshape(rows_here, length, model_width))
    attn_out = low_back(jnp.einsum('rle,ed->rld', mixed, w_output, precision=highest))
    middle = inputs + attn_out
    normed_ffn = low(middle * rms_scale(middle) * gain_ffn)
    gate_proj = low_back(jnp.einsum('rld,df->rlf', normed_ffn, w_gate, precision=highest))
    up_proj = low_back(jnp.einsum('rld,df->rlf', normed_ffn, w_up, precision=highest))
    hidden = low(jax.nn.gelu(gate_proj, approximate=True) * up_proj)
    ffn_out = low_back(jnp.einsum('rlf,fd->rld', hidden, w_down, precision=highest))
    output = middle + ffn_out
    final_norm = output * rms_scale(output) * gain_final
    member = (segment[:, None, :] == jnp.arange(1, ITEMS + 1, dtype=jnp.int32)[None, :, None]).astype(jnp.float32)
    counts = lax.optimization_barrier(jnp.sum(member, axis=-1, keepdims=True))
    pooled = jnp.einsum('rkl,rld->rkd', member, final_norm, precision=highest) / counts
    unit_vec = low(pooled * lax.rsqrt(lax.optimization_barrier(jnp.sum(pooled * pooled, axis=-1, keepdims=True)) + eps_norm))
    return (output, unit_vec)

def reference(tokens, segments, w_query, w_key, w_value, w_output, w_gate, w_up, w_down, gain_attn, gain_ffn, gain_final, bias_table, out_grad, score_grad):
    params = (w_query.astype(jnp.float32), w_key.astype(jnp.float32), w_value.astype(jnp.float32), w_output.astype(jnp.float32), w_gate.astype(jnp.float32), w_up.astype(jnp.float32), w_down.astype(jnp.float32), gain_attn, gain_ffn, gain_final, bias_table)
    rows_all = 2 * ROWS
    group_rows = math.gcd(rows_all, max(1, 4096 // L))
    flat_in = tokens.astype(jnp.float32).reshape(rows_all // group_rows, group_rows, L, D)
    flat_seg = segments.reshape(rows_all // group_rows, group_rows, L)

    def forward(weights_all, inputs):

        def one_block(block_pair):
            return block_layer(weights_all, block_pair[0], block_pair[1])
        outputs, units = lax.map(jax.checkpoint(one_block), (inputs, flat_seg))
        units = units.reshape(2, ROWS * ITEMS, D)
        scores = jnp.dot(units[0], units[1].T, precision=highest) / temper
        return (outputs.reshape(2, ROWS, L, D), scores)
    (outputs, scores), pullback = jax.vjp(forward, params, flat_in)
    param_grads, input_grads = pullback((out_grad.astype(jnp.float32), score_grad))
    return (outputs.astype(jnp.bfloat16), scores, input_grads.reshape(2, ROWS, L, D).astype(jnp.bfloat16), param_grads[0], param_grads[1], param_grads[2], param_grads[3], param_grads[4], param_grads[5], param_grads[6], param_grads[7], param_grads[8], param_grads[9], param_grads[10])
```

```python
import functools

import jax
import jax.numpy as jnp
import numpy as np
from jax import lax
from jax.experimental import pallas as pl
from jax.experimental.pallas import tpu as pltpu
from jax.sharding import PartitionSpec as P

ITEMS = 8
eps_norm = 1e-06
temper = 0.05
max_distance = 128
highest = lax.Precision.HIGHEST
masked_value = -1000000000.0
contract_rows = (((0,), (0,)), ((), ()))
contract_cols = (((1,), (1,)), ((), ()))
f32 = jnp.float32
bf16 = jnp.bfloat16
LANES = 128
VMEM_BYTES = 56 * 1024 * 1024
TINY = pl.CostEstimate(flops=1024, bytes_accessed=1024, transcendentals=0)


def bucket_of(relative, bucket_count):
    halfway = bucket_count // 2
    upper_part = np.where(relative > 0, halfway, 0)
    distance = np.abs(relative)
    exact_span = halfway // 2
    scaled = (
        np.log(np.maximum(distance, 1) / exact_span)
        / np.log(max_distance / exact_span)
        * (halfway - exact_span)
    )
    far_bucket = np.minimum(
        exact_span + np.floor(np.maximum(scaled, 0.0)).astype(np.int32), halfway - 1
    )
    return (upper_part + np.where(distance < exact_span, distance, far_bucket)).astype(np.int32)


def one_hot(buckets, bucket_count):
    return (buckets[:, None] == np.arange(bucket_count)[None, :]).astype(np.float32)


def near_offsets():
    lane = np.arange(4 * LANES)
    return np.where(lane < 3 * LANES, lane - LANES, lane - 5 * LANES)


def rms_scale(values):
    return lax.rsqrt(jnp.mean(values * values, axis=-1, keepdims=True) + eps_norm)


def norm_back(values, scale, gain, grad_normed):
    scaled_grad = grad_normed * gain
    grad_values = scale * scaled_grad - values * scale**3 * jnp.mean(
        scaled_grad * values, axis=-1, keepdims=True
    )
    grad_gain = jnp.sum(grad_normed * values * scale, axis=0, keepdims=True)
    return (grad_values, grad_gain)


def project(left, right):
    return jnp.dot(left, right, preferred_element_type=f32)


def dot_f32(left, right, dims):
    return lax.dot_general(left, right, dims, preferred_element_type=f32)


def dot_exact(left, right):
    return jnp.dot(left, right, precision=highest, preferred_element_type=f32)


def params(**more):
    return pltpu.CompilerParams(vmem_limit_bytes=VMEM_BYTES, **more)


def shape_of(dims, kind):
    return jax.ShapeDtypeStruct(dims, kind)


def whole(array):
    zeros = (0,) * len(array.shape)
    return pl.BlockSpec(array.shape, lambda *_: zeros)


def half_lanes(block, side):
    lane = lax.broadcasted_iota(jnp.int32, block.shape, 1)
    keep = lane < LANES // 2 if side == 0 else lane >= LANES // 2
    return jnp.where(keep, block, jnp.zeros_like(block))


def attn_fwd_kernel(
    x_ref, gain_a_ref, gain_f_ref, wq_ref, wk_ref, wv_ref, wo_ref, seg_col_ref, seg_row_ref, base_ref,
    normed_ref, q_ref, k_ref, v_ref, probs_ref, mixed_ref, middle_ref, normed_ffn_ref,
):
    step = pl.program_id(0)
    length = x_ref.shape[0]
    blocks = length // LANES

    @pl.when(step == 0)
    def _():
        x = x_ref[...].astype(f32)
        normed_ref[...] = (x * rms_scale(x) * gain_a_ref[...]).astype(bf16)
        middle_ref[...] = x

    normed = normed_ref[...]
    query = project(normed, wq_ref[...]).astype(bf16)
    key = project(normed, wk_ref[...]).astype(bf16)
    value = project(normed, wv_ref[...]).astype(bf16)
    q_ref[...] = query
    k_ref[...] = key
    v_ref[...] = value
    near, far = [], []
    for side in range(2):
        base = base_ref[0, side : side + 1, :]
        spread = jnp.broadcast_to(base, (LANES, 4 * LANES))
        near.append(pltpu.roll(spread, 0, 1, stride=1, stride_axis=0))
        far.append((base[:, 3 * LANES + 1 : 3 * LANES + 2], base[:, 3 * LANES - 1 : 3 * LANES]))
    for ib in range(blocks):
        rows = slice(ib * LANES, (ib + 1) * LANES)
        same = seg_col_ref[rows, :] == seg_row_ref[...]
        out = []
        for side in range(2):
            logits = dot_f32(half_lanes(query[rows, :], side), key, contract_cols)
            tiles = []
            for jb in range(blocks):
                if jb - ib < -1:
                    tile = jnp.broadcast_to(far[side][0], (LANES, LANES))
                elif jb - ib > 1:
                    tile = jnp.broadcast_to(far[side][1], (LANES, LANES))
                else:
                    at = (jb - ib + 1) * LANES
                    tile = near[side][:, at : at + LANES]
                tiles.append(tile)
            logits = jnp.where(same, logits + jnp.concatenate(tiles, axis=1), masked_value)
            peak = jnp.max(logits, axis=1, keepdims=True)
            weight = jnp.exp(logits - peak)
            total = jnp.sum(weight, axis=1, keepdims=True)
            probs = (weight * (1.0 / total)).astype(bf16)
            probs_ref[side, rows, :] = probs
            out.append(project(probs, value))
        lane = lax.broadcasted_iota(jnp.int32, (LANES, LANES), 1)
        mixed_ref[rows, :] = jnp.where(lane < LANES // 2, out[0], out[1]).astype(bf16)
    middle_ref[...] += project(mixed_ref[...], wo_ref[...])

    @pl.when(step == pl.num_programs(0) - 1)
    def _():
        middle = middle_ref[...]
        normed_ffn_ref[...] = (middle * rms_scale(middle) * gain_f_ref[...]).astype(bf16)


def attn_fwd(x, gain_a, gain_f, w_query, w_key, w_value, w_output, seg_col, seg_row, base):
    length, width = x.shape
    pairs = width // LANES
    pair = pl.BlockSpec((length, LANES), lambda h: (0, h))
    column = pl.BlockSpec((width, LANES), lambda h: (0, h))
    low = shape_of((length, width), bf16)
    high = shape_of((length, width), f32)
    base = base.reshape(pairs, 2, 4 * LANES)
    return pl.pallas_call(
        attn_fwd_kernel,
        grid=(pairs,),
        in_specs=[
            whole(x),
            whole(gain_a),
            whole(gain_f),
            column,
            column,
            column,
            pl.BlockSpec((LANES, width), lambda h: (h, 0)),
            whole(seg_col),
            whole(seg_row),
            pl.BlockSpec((1, 2, 4 * LANES), lambda h: (h, 0, 0)),
        ],
        out_specs=[
            whole(low),
            pair,
            pair,
            pair,
            pl.BlockSpec((2, length, length), lambda h: (h, 0, 0)),
            pair,
            whole(high),
            whole(low),
        ],
        out_shape=[low, low, low, low, shape_of((2 * pairs, length, length), bf16), low, high, low],
        compiler_params=params(),
        cost_estimate=TINY,
        name="attn_fwd",
    )(x, gain_a, gain_f, w_query, w_key, w_value, w_output, seg_col, seg_row, base)


def attn_bwd_kernel(q_ref, k_ref, v_ref, g_ref, probs_ref, gq_ref, gk_ref, gv_ref, sums_ref, grad_scr):
    length = q_ref.shape[0]
    blocks = length // LANES
    key = k_ref[...]
    value = v_ref[...]
    gq, gk, gv, sums = [], [], [], []
    row = lax.broadcasted_iota(jnp.int32, (LANES, LANES), 0)
    column = lax.broadcasted_iota(jnp.int32, (LANES, LANES), 1)
    flip = (row + column == LANES - 1).astype(f32)
    for side in range(2):
        near = [None, None, None]
        far = [None, None]
        parts = []
        for ib in range(blocks):
            rows = slice(ib * LANES, (ib + 1) * LANES)
            grad_mixed = half_lanes(g_ref[rows, :], side)
            grad_probs = dot_f32(grad_mixed, value, contract_cols)
            probs = probs_ref[side, rows, :].astype(f32)
            inner = jnp.sum(probs * grad_probs, axis=1, keepdims=True)
            grad_low = (probs * (grad_probs - inner)).astype(bf16)
            grad_scr[rows, :] = grad_low
            parts.append(project(grad_low, key))
            wide = grad_low.astype(f32)
            for jb in range(blocks):
                tile = wide[:, jb * LANES : (jb + 1) * LANES]
                if abs(jb - ib) <= 1:
                    into, at = near, jb - ib + 1
                else:
                    into, at = far, 0 if jb < ib else 1
                into[at] = tile if into[at] is None else into[at] + tile
        gq.append(jnp.concatenate(parts, axis=0))
        half = slice(side * LANES // 2, (side + 1) * LANES // 2)
        gk.append(project(q_ref[...].T[half, :], grad_scr[...]))
        gv.append(project(g_ref[...].T[half, :], probs_ref[side]))
        spread = dot_exact(flip, jnp.concatenate(near, axis=1))
        spread = jnp.concatenate([spread, jnp.zeros_like(near[0])], axis=1)
        skew = pltpu.roll(spread, 0, 1, stride=1, stride_axis=0)
        sums.append(jnp.sum(skew, axis=0, keepdims=True))
        lows = [jnp.sum(tile, axis=0, keepdims=True) for tile in far]
        sums.append(jnp.concatenate(lows + [jnp.zeros((1, 2 * LANES), f32)], axis=1))
    lane = lax.broadcasted_iota(jnp.int32, (length, LANES), 1)
    gq_ref[...] = jnp.where(lane < LANES // 2, gq[0], gq[1]).astype(bf16)
    gk_ref[...] = jnp.concatenate(gk, axis=0).astype(bf16).T
    gv_ref[...] = jnp.concatenate(gv, axis=0).astype(bf16).T
    sums_ref[0] = jnp.concatenate(sums, axis=0)


def attn_bwd(query, key, value, grad_mixed, probs):
    length, width = query.shape
    pairs = width // LANES
    pair = pl.BlockSpec((length, LANES), lambda h: (0, h))
    low = shape_of((length, width), bf16)
    return pl.pallas_call(
        attn_bwd_kernel,
        grid=(pairs,),
        in_specs=[pair, pair, pair, pair, pl.BlockSpec((2, length, length), lambda h: (h, 0, 0))],
        out_specs=[pair, pair, pair, pl.BlockSpec((1, 4, 4 * LANES), lambda h: (h, 0, 0))],
        out_shape=[low, low, low, shape_of((pairs, 4, 4 * LANES), f32)],
        scratch_shapes=[pltpu.VMEM((length, length), bf16)],
        compiler_params=params(),
        cost_estimate=TINY,
        name="attn_bwd",
    )(query, key, value, grad_mixed, probs)


def attn_in_kernel(
    gq_ref, gk_ref, gv_ref, wq_ref, wk_ref, wv_ref, x_ref, middle_ref, gain_ref, sums_ref, near_ref, far_ref,
    gain_f_ref, gain_l_ref, tokens_ref, small_ref,
):
    grad_normed = dot_f32(gq_ref[...], wq_ref[...], contract_cols)
    grad_normed += dot_f32(gk_ref[...], wk_ref[...], contract_cols)
    grad_normed += dot_f32(gv_ref[...], wv_ref[...], contract_cols)
    x = x_ref[...].astype(f32)
    grad_in, grad_gain = norm_back(x, rms_scale(x), gain_ref[...], grad_normed)
    tokens_ref[...] = (middle_ref[...] + grad_in).astype(bf16)
    heads = sums_ref.shape[0]
    table = dot_exact(sums_ref[:, 0, :], near_ref[...]) + dot_exact(sums_ref[:, 1, :], far_ref[...])
    each = x_ref.shape[1] // LANES
    small_ref[...] = jnp.zeros_like(small_ref)
    for index, gain in enumerate((grad_gain, gain_f_ref[...], gain_l_ref[...])):
        for r in range(each):
            small_ref[index * each + r : index * each + r + 1, :] = gain[:, r * LANES : (r + 1) * LANES]
    small_ref[3 * each : 3 * each + heads, :] = table


def attn_in(gq, gk, gv, w_query, w_key, w_value, x, grad_middle, gain, sums, near_hot, far_hot, gain_f, gain_l):
    args = (gq, gk, gv, w_query, w_key, w_value, x, grad_middle, gain, sums, near_hot, far_hot, gain_f, gain_l)
    rows = 3 * (x.shape[1] // LANES) + sums.shape[0]
    outs = [shape_of(x.shape, bf16), shape_of((-(-rows // 8) * 8, LANES), f32)]
    return pl.pallas_call(
        attn_in_kernel,
        grid=(1,),
        in_specs=[whole(a) for a in args],
        out_specs=[whole(o) for o in outs],
        out_shape=outs,
        compiler_params=params(),
        cost_estimate=TINY,
        name="attn_in",
    )(*args)


def gelu_parts(gate):
    c = np.float32(np.sqrt(2.0 / np.pi))
    cube = np.float32(0.044715 * np.sqrt(2.0 / np.pi))
    square = gate * gate
    half = 0.5 * jnp.tanh(gate * (c + cube * square)) + 0.5
    act = gate * half
    slope = half + act * (1.0 - half) * (2 * c + 6 * cube * square)
    return act, slope


def ffn_fwd_kernel(
    normed_ref, middle_ref, wg_ref, wu_ref, wd_ref, seg_row_ref, gain_ref, score_ref,
    hidden_ref, act_ref, coef_ref, full_ref, out_ref, pooled_ref, pack_ref,
):
    step = pl.program_id(0)

    @pl.when(step == 0)
    def _():
        full_ref[...] = middle_ref[...]

    normed = normed_ref[...]
    gate = project(normed, wg_ref[...])
    up = project(normed, wu_ref[...])
    act, slope = gelu_parts(gate)
    hidden = (act * up).astype(bf16)
    hidden_ref[...] = hidden
    act_ref[...] = act.astype(bf16)
    coef_ref[...] = (up * slope).astype(bf16)
    full_ref[...] += project(hidden, wd_ref[...])

    @pl.when(step == pl.num_programs(0) - 1)
    def _():
        full = full_ref[...]
        out_ref[...] = full.astype(bf16)
        final_norm = full * rms_scale(full) * gain_ref[...]
        item = lax.broadcasted_iota(jnp.int32, (ITEMS, full.shape[0]), 0) + 1
        member = (item == seg_row_ref[...]).astype(f32)
        pooled = dot_exact(member, final_norm) / jnp.sum(member, axis=1, keepdims=True)
        pooled_ref[...] = pooled
        inv_length = lax.rsqrt(jnp.sum(pooled * pooled, axis=1, keepdims=True) + eps_norm)
        parts = [(pooled * inv_length).astype(bf16)]
        rest = score_ref[...]
        for _ in range(3):
            parts.append(rest.astype(bf16))
            rest = rest - parts[-1].astype(f32)
        pack = jnp.concatenate(parts, axis=1)
        for b in range(pack_ref.shape[0]):
            pack_ref[b] = pack


def ffn_fwd(normed, middle, w_gate, w_up, w_down, seg_row, gain, score_grad, n, block=512):
    length, width = normed.shape
    wide = w_gate.shape[1]
    weight = pl.BlockSpec((width, block), lambda j: (0, j))
    column = pl.BlockSpec((length, block), lambda j: (0, j))
    low = shape_of((length, wide), bf16)
    outs = [
        low,
        low,
        low,
        shape_of((length, width), f32),
        shape_of((length, width), bf16),
        shape_of((ITEMS, width), f32),
        shape_of((n, ITEMS, width + 3 * score_grad.shape[1]), bf16),
    ]
    return pl.pallas_call(
        ffn_fwd_kernel,
        grid=(wide // block,),
        in_specs=[
            whole(normed),
            whole(middle),
            weight,
            weight,
            pl.BlockSpec((block, width), lambda j: (j, 0)),
            whole(seg_row),
            whole(gain),
            whole(score_grad),
        ],
        out_specs=[column, column, column] + [whole(o) for o in outs[3:]],
        out_shape=outs,
        compiler_params=params(),
        cost_estimate=TINY,
        name="ffn_fwd",
    )(normed, middle, w_gate, w_up, w_down, seg_row, gain, score_grad)


def ffn_back_kernel(
    at_ref, own_ref, got_ref, full_ref, og_ref, pooled_ref, seg_col_ref, seg_row_ref, gain_ref, wd_ref, act_ref, coef_ref,
    scores_ref, ffn_grad_ref, grad_out_ref, gain_l_ref, keep_ref, send_ref, units_scr, turned_scr,
):
    step = pl.program_id(0)
    tower = at_ref[0]
    me = at_ref[1]
    length, width = full_ref.shape
    n = own_ref.shape[0]

    @pl.when(step == 0)
    def _():
        items = n * ITEMS
        for b in range(n):
            units_scr[b * ITEMS : (b + 1) * ITEMS, :] = got_ref[b, :, :width].astype(f32)
        theirs = units_scr[...].astype(bf16)
        for b in range(n):
            rows = slice(b * ITEMS, (b + 1) * ITEMS)
            units_scr[rows, :] = own_ref[b, :, :width].astype(f32)
            turned_scr[rows, :] = sum(
                own_ref[b, :, width + k * items : width + (k + 1) * items].astype(f32) for k in range(3)
            )
        ours = units_scr[...].astype(bf16)
        queries = jnp.where(tower == 0, ours, theirs)
        docs = jnp.where(tower == 0, theirs, ours)
        units_scr[...] = queries.astype(f32)
        mine = pl.ds(pl.multiple_of(me * ITEMS, ITEMS), ITEMS)
        scores_ref[...] = dot_f32(units_scr[mine, :].astype(bf16), docs, contract_cols) / temper
        score_grad = turned_scr[...]
        turned_scr[...] = jnp.where(tower == 0, score_grad, score_grad.T)
        grad_unit = dot_exact(turned_scr[mine, :], theirs.astype(f32)) / temper
        pooled = pooled_ref[...]
        inv_length = lax.rsqrt(jnp.sum(pooled * pooled, axis=1, keepdims=True) + eps_norm)
        grad_pooled = inv_length * grad_unit - pooled * inv_length**3 * jnp.sum(
            grad_unit * pooled, axis=1, keepdims=True
        )
        item = lax.broadcasted_iota(jnp.int32, (ITEMS, length), 0) + 1
        count = jnp.sum((item == seg_row_ref[...]).astype(f32), axis=1, keepdims=True)
        item = lax.broadcasted_iota(jnp.int32, (length, ITEMS), 1) + 1
        grad_final = dot_exact((item == seg_col_ref[...]).astype(f32), grad_pooled / count)
        full = full_ref[...]
        back, gain_l_ref[...] = norm_back(full, rms_scale(full), gain_ref[...], grad_final)
        grad_output = og_ref[...].astype(f32) + back
        grad_out_ref[...] = grad_output
        ffn_grad_ref[...] = grad_output.astype(bf16)

    grad_hidden = dot_f32(ffn_grad_ref[...], wd_ref[...], contract_cols)
    grad_gate = (grad_hidden * coef_ref[...].astype(f32)).astype(bf16)
    grad_up = (grad_hidden * act_ref[...].astype(f32)).astype(bf16)

    @pl.when(tower == 0)
    def _():
        keep_ref[...] = grad_gate
        send_ref[...] = grad_up

    @pl.when(tower != 0)
    def _():
        keep_ref[...] = grad_up
        send_ref[...] = grad_gate


def ffn_back(at, own, got, full, out_grad, pooled, seg_col, seg_row, gain, w_down, act, coef, block=512):
    length, width = full.shape
    wide = act.shape[1]
    n = own.shape[0]
    items = n * ITEMS
    column = pl.BlockSpec((length, block), lambda j, s: (0, j))
    low = shape_of((length, wide), bf16)
    outs = [
        shape_of((ITEMS, items), f32),
        shape_of((length, width), bf16),
        shape_of((length, width), f32),
        shape_of((1, width), f32),
        low,
        low,
    ]
    args = (own, got, full, out_grad, pooled, seg_col, seg_row, gain)
    return pl.pallas_call(
        ffn_back_kernel,
        grid_spec=pltpu.PrefetchScalarGridSpec(
            num_scalar_prefetch=1,
            grid=(wide // block,),
            in_specs=[whole(a) for a in args]
            + [pl.BlockSpec((block, width), lambda j, s: (j, 0)), column, column],
            out_specs=[whole(o) for o in outs[:4]] + [column, column],
            scratch_shapes=[pltpu.VMEM((items, width), f32), pltpu.VMEM((items, items), f32)],
        ),
        out_shape=outs,
        compiler_params=params(),
        cost_estimate=TINY,
        name="ffn_back",
    )(at, *args, w_down, act, coef)


def mid_back_kernel(
    at_ref, keep_ref, send_ref, wg_ref, wu_ref, middle_ref, gain_ref, grad_out_ref, wo_ref,
    grad_middle_ref, attn_grad_ref, grad_mixed_ref, gain_f_ref, total_scr,
):
    step = pl.program_id(0)
    first = at_ref[0] == 0
    keep = keep_ref[...]
    send = send_ref[...]
    term = dot_f32(jnp.where(first, keep, send), wg_ref[...], contract_cols)
    term += dot_f32(jnp.where(first, send, keep), wu_ref[...], contract_cols)

    @pl.when(step == 0)
    def _():
        total_scr[...] = term

    @pl.when(step != 0)
    def _():
        total_scr[...] += term

    @pl.when(step == pl.num_programs(0) - 1)
    def _():
        middle = middle_ref[...]
        back, gain_f_ref[...] = norm_back(middle, rms_scale(middle), gain_ref[...], total_scr[...])
        grad_middle = grad_out_ref[...] + back
        grad_middle_ref[...] = grad_middle
        attn_grad = grad_middle.astype(bf16)
        attn_grad_ref[...] = attn_grad
        grad_mixed_ref[...] = dot_f32(attn_grad, wo_ref[...], contract_cols).astype(bf16)


def mid_back(at, keep, send, w_gate, w_up, middle, gain, grad_output, w_output, block=512):
    length, width = middle.shape
    wide = keep.shape[1]
    column = pl.BlockSpec((length, block), lambda j, s: (0, j))
    weight = pl.BlockSpec((width, block), lambda j, s: (0, j))
    outs = [
        shape_of((length, width), f32),
        shape_of((length, width), bf16),
        shape_of((length, width), bf16),
        shape_of((1, width), f32),
    ]
    args = (middle, gain, grad_output, w_output)
    return pl.pallas_call(
        mid_back_kernel,
        grid_spec=pltpu.PrefetchScalarGridSpec(
            num_scalar_prefetch=1,
            grid=(wide // block,),
            in_specs=[column, column, weight, weight] + [whole(a) for a in args],
            out_specs=[whole(o) for o in outs],
            scratch_shapes=[pltpu.VMEM((length, width), f32)],
        ),
        out_shape=outs,
        compiler_params=params(),
        cost_estimate=TINY,
        name="mid_back",
    )(at, keep, send, w_gate, w_up, *args)


def reversed_bits(value, count):
    out = 0
    for k in range(count):
        out = out | (((value >> k) & 1) << (count - 1 - k))
    return out


def bit_order(first, bits):
    return [first, 1 - first] + list(range(2, bits))


def grad_pieces(mats, pieces, n, at):
    bits = n.bit_length() - 1
    widths = [lefts[0].shape[1] // n for lefts, _, _, _ in mats]
    inner = None
    if all(w % 16 == 0 for w in widths):
        for cand in (4, 8, 16, 32):
            if cand <= n and all(cand * w % LANES == 0 for w in widths):
                inner = cand
                break
    if inner is None:
        return grad_pieces_plain(mats, pieces, n, at)
    groups = n // inner
    inner_count = inner.bit_length() - 1
    flat, in_specs, counts, spans = [], [], [], []
    for (lefts, rights, halved, _), width in zip(mats, widths):
        for left in lefts:
            flat.append(left)
            in_specs.append(pl.BlockSpec((left.shape[0], inner * width), lambda g, m: (0, g)))
        for right in rights:
            flat.append(right)
            span = right.shape[1] // 2 if halved else right.shape[1]
            if halved:
                in_specs.append(pl.BlockSpec((right.shape[0], span), lambda g, m: (0, m[0])))
            else:
                in_specs.append(whole(right))
        counts.append(len(lefts))
        spans.append(span)

    def place(g, m):
        return (0, reversed_bits(g ^ (m[1] // inner), bits - inner_count), 0, 0)

    out_shape, out_specs = [], []
    for _, rows, lanes in pieces:
        for _ in range(2):
            out_shape.append(shape_of((inner // 2, groups, rows, lanes), bf16))
            out_specs.append(pl.BlockSpec((inner // 2, 1, rows, lanes), place))
    dests = [d for _, _, _, d in mats]
    scratch = [pltpu.VMEM((inner, w, span), bf16) for w, span in zip(widths, spans)]

    def kernel(at_ref, *refs):
        ins = refs[: len(flat)]
        outs = refs[len(flat) : len(flat) + len(out_shape)]
        scrs = refs[len(flat) + len(out_shape) :]
        own = at_ref[1] % inner
        at_in = 0
        for index, count in enumerate(counts):
            total = None
            for k in range(count):
                term = dot_f32(ins[at_in + k][...], ins[at_in + count + k][...], contract_rows)
                total = term if total is None else total + term
            at_in += 2 * count
            low = total.astype(bf16)
            width = widths[index]
            for i in range(inner):
                scrs[index][i] = low[i * width : (i + 1) * width]
            for piece, offset, lanes in dests[index]:
                first = pieces[piece][0]
                order = bit_order(first, inner_count)
                for slot in range(inner):
                    pos = sum(((slot >> (inner_count - 1 - k)) & 1) << bit for k, bit in enumerate(order))
                    out = outs[2 * piece + (0 if slot >= inner // 2 else 1)]
                    out[slot % (inner // 2), 0, offset : offset + width, :] = scrs[index][pos ^ own][:, lanes]

    res = pl.pallas_call(
        kernel,
        grid_spec=pltpu.PrefetchScalarGridSpec(
            num_scalar_prefetch=1,
            grid=(groups,),
            in_specs=in_specs,
            out_specs=out_specs,
            scratch_shapes=scratch,
        ),
        out_shape=out_shape,
        compiler_params=params(),
        cost_estimate=TINY,
        name="weight_grads",
    )(at, *flat)
    found = []
    for index, (first, rows, lanes) in enumerate(pieces):
        found.append((res[2 * index], res[2 * index + 1], bit_order(first, bits)[1:]))
    return found


def grad_pieces_plain(mats, pieces, n, at):
    bits = n.bit_length() - 1
    order = jnp.arange(n, dtype=jnp.int32) ^ at[1]
    filled = [[] for _ in pieces]
    for lefts, rights, halved, dests in mats:
        if halved:
            span = rights[0].shape[1] // 2
            rights = [lax.dynamic_slice_in_dim(r, at[0] * span, span, 1) for r in rights]
        total = sum(dot_f32(a, b, contract_rows) for a, b in zip(lefts, rights)).astype(bf16)
        total = jnp.take(total.reshape(n, -1, total.shape[1]), order, axis=0)
        for piece, offset, lanes in dests:
            filled[piece].append((offset, total[:, :, lanes]))
    found = []
    for (first, rows, lanes), parts in zip(pieces, filled):
        parts = [p for _, p in sorted(parts, key=lambda p: p[0])]
        joined = jnp.concatenate(parts, axis=1)
        tail = joined.shape[1:]
        sequence = bit_order(first, bits)
        joined = joined.reshape((2,) * bits + tail)
        joined = joined.transpose([bits - 1 - b for b in sequence] + [bits, bits + 1])
        found.append((joined[1], joined[0], sequence[1:]))
    return found


def swap(values, bit, n):
    return lax.ppermute(values, "batch", [(i, i ^ (1 << bit)) for i in range(n)])


def swap_tower(values):
    return lax.ppermute(values, "tower", [(0, 1), (1, 0)])


def after(values, *others):
    return lax.optimization_barrier((values,) + others)[0]


class Part:
    def __init__(self, held, bits):
        self.held = held
        self.bits = bits

    def total(self, which):
        return sum(h[which].astype(f32) for h in self.held)


def open_pieces(pieces, firsts, n):
    parts = []
    for (send, keep, bits), first in zip(pieces, firsts):
        shape = (2,) * len(bits) + send.shape[-2:]
        got = swap(send, first, n)
        parts.append(Part([keep.reshape(shape), got.reshape(shape)], bits))
    return parts


def to_send(parts):
    return [part.total(1).astype(bf16) for part in parts]


def exchange(parts, sends, n):
    return [
        Part([h[0] for h in part.held] + [swap(send, part.bits[0], n)], part.bits[1:])
        for part, send in zip(parts, sends)
    ]


def to_send_joined(parts, dim):
    return jnp.concatenate(to_send(parts), axis=dim)


def exchange_joined(parts, send, dim, n):
    got = swap(send, parts[0].bits[0], n)
    at, found = 0, []
    for part in parts:
        size = part.held[0].shape[dim]
        piece = lax.slice_in_dim(got, at, at + size, axis=got.ndim + dim)
        found.append(Part([h[0] for h in part.held] + [piece], part.bits[1:]))
        at += size
    return found


def hold(parts, *others):
    return [Part(part.held[:-1] + [after(part.held[-1], *others)], part.bits) for part in parts]


def finish(parts, dim):
    return jnp.concatenate([sum(h.astype(f32) for h in part.held) for part in parts], axis=dim).astype(bf16)


def body(
    n,
    tokens,
    segments,
    w_query,
    w_key,
    w_value,
    w_output,
    w_gate,
    w_up,
    w_down,
    gain_attn,
    gain_ffn,
    gain_final,
    bias_table,
    out_grad,
    score_grad,
):
    length = tokens.shape[2]
    width = tokens.shape[3]
    wide = w_gate.shape[1]
    heads = bias_table.shape[1]
    buckets = bias_table.shape[0]
    bits = n.bit_length() - 1
    half = width // 2
    quarter = wide // 4
    narrow = width // n
    tower = lax.axis_index("tower")
    at = jnp.stack([tower, lax.axis_index("batch")]).astype(jnp.int32)
    x = tokens.reshape(length, width)
    seg_col = segments.reshape(length, 1)
    seg_row = segments.reshape(1, length)
    gain_attn = gain_attn.reshape(1, width)
    gain_ffn = gain_ffn.reshape(1, width)
    gain_final = gain_final.reshape(1, width)

    near_hot = jnp.asarray(one_hot(bucket_of(near_offsets(), buckets), buckets))
    base = lax.dot_general(bias_table, near_hot, (((0,), (1,)), ((), ())), precision=highest)
    normed, query, key, value, probs, mixed, middle, normed_ffn = attn_fwd(
        x, gain_attn, gain_ffn, w_query, w_key, w_value, w_output, seg_col, seg_row, base
    )
    hidden, act, coef, full, output, pooled, pack = ffn_fwd(
        normed_ffn, middle, w_gate, w_up, w_down, seg_row, gain_final, score_grad, n
    )
    packs = lax.all_to_all(pack, "batch", 0, 0, tiled=True)
    normed_got = swap_tower(normed)
    mixed_got = swap_tower(mixed)
    ffn_got = swap_tower(normed_ffn)
    hidden_got = swap_tower(hidden)
    packs_got = swap_tower(packs)
    packs_got = after(packs_got, normed_got, mixed_got, ffn_got, hidden_got)

    scores, ffn_grad, grad_output, grad_gain_final, pair_own, pair_send = ffn_back(
        at, packs, packs_got, full, out_grad.reshape(length, width), pooled, seg_col, seg_row, gain_final, w_down, act, coef
    )
    ffn_grad_got = swap_tower(ffn_grad)
    pair_got = swap_tower(pair_send)

    down = grad_pieces(
        [
            (
                [ffn_grad, ffn_grad_got],
                [hidden, hidden_got],
                True,
                [(0, 0, slice(0, quarter)), (1, 0, slice(quarter, 2 * quarter))],
            )
        ],
        [(0, narrow, quarter), (1, narrow, quarter)],
        n,
        at,
    )
    down_parts = open_pieces(down, (0, 1), n)
    pair_got = after(pair_got, down[0][0], down[1][0])
    wide_grads = grad_pieces(
        [
            (
                [pair_own, pair_got],
                [normed_ffn, ffn_got],
                False,
                [(0, 0, slice(0, half)), (1, 0, slice(half, width))],
            )
        ],
        [(0, wide // n, half), (1, wide // n, half)],
        n,
        at,
    )

    down_parts = hold(down_parts, wide_grads[0][0])
    sends = to_send(down_parts)
    wide_parts = open_pieces([(after(w[0], *sends),) + w[1:] for w in wide_grads], (0, 1), n)
    down_parts = exchange(down_parts, sends, n)
    grad_middle, attn_grad, grad_mixed, grad_gain_ffn = mid_back(
        at, after(pair_own, *sends), pair_send, w_gate, w_up, middle, gain_ffn, grad_output, w_output
    )
    attn_grad_got = swap_tower(attn_grad)
    grad_query, grad_key, grad_value, sums = attn_bwd(query, key, value, grad_mixed, probs)
    grad_query_got = swap_tower(grad_query)
    grad_key_got = swap_tower(grad_key)
    grad_value_got = swap_tower(grad_value)
    wide_parts = hold(wide_parts, grad_query)
    sends = to_send(wide_parts)
    wide_parts = exchange(wide_parts, sends, n)
    down_parts = hold(down_parts, *sends)
    send = to_send_joined(down_parts, -1)
    down_parts = exchange_joined(down_parts, send, -1, n)
    attn = grad_pieces(
        [
            ([grad_query, grad_query_got], [normed, normed_got], True, [(0, 0, slice(0, half))]),
            ([grad_key, grad_key_got], [normed, normed_got], True, [(0, narrow, slice(0, half))]),
            ([grad_value, after(grad_value_got, send)], [normed, normed_got], True, [(1, 0, slice(0, half))]),
            ([attn_grad, attn_grad_got], [mixed, mixed_got], True, [(1, narrow, slice(0, half))]),
        ],
        [(0, 2 * narrow, half), (1, 2 * narrow, half)],
        n,
        at,
    )
    attn_parts = open_pieces(attn, (0, 1), n)
    wide_parts = hold(wide_parts, attn[0][0])
    send = to_send_joined(wide_parts, -1)
    wide_parts = exchange_joined(wide_parts, send, -1, n)
    down_parts = hold(down_parts, send)
    send = to_send_joined(down_parts, -1)
    down_parts = exchange_joined(down_parts, send, -1, n)

    near_sums = jnp.asarray(
        np.pad(one_hot(bucket_of(np.arange(4 * LANES) - (2 * LANES - 1), buckets), buckets), ((0, 0), (0, LANES - buckets)))
    )
    far_sums = np.zeros((4 * LANES, LANES), np.float32)
    far_sums[:LANES, buckets // 2 - 1] = 1.0
    far_sums[LANES : 2 * LANES, buckets - 1] = 1.0
    grad_tokens, small = attn_in(
        after(grad_query, send), grad_key, grad_value, w_query, w_key, w_value, x, grad_middle, gain_attn,
        sums.reshape(heads, 2, 4 * LANES), near_sums, jnp.asarray(far_sums), grad_gain_ffn, grad_gain_final,
    )
    attn_parts = hold(attn_parts, grad_tokens)
    sends = to_send(attn_parts)
    attn_parts = exchange(attn_parts, sends, n)
    small = after(small, *sends) + swap_tower(small)
    small = jnp.broadcast_to(small[None], (n,) + small.shape)
    wide_parts = hold(wide_parts, small)
    last = small
    while wide_parts[0].bits:
        send = to_send_joined(wide_parts, -1)
        wide_parts = exchange_joined(wide_parts, send, -1, n)
        if down_parts[0].bits:
            down_parts = hold(down_parts, send)
            send = to_send_joined(down_parts, -1)
            down_parts = exchange_joined(down_parts, send, -1, n)
        attn_parts = hold(attn_parts, send)
        send = to_send_joined(attn_parts, -2)
        attn_parts = exchange_joined(attn_parts, send, -2, n)
        last = send
        if wide_parts[0].bits:
            wide_parts = hold(wide_parts, last)
    small = lax.all_to_all(after(small, last), "batch", 0, 0, tiled=True)
    down_own = finish(hold(down_parts, last), -1)
    wide_own = finish(hold(wide_parts, down_own), -1)
    small = jnp.sum(after(small, wide_own), axis=0)
    each = width // LANES
    gains = small[: 3 * each].reshape(3, width)
    gains = lax.dynamic_slice_in_dim(gains, at[1] * narrow, narrow, 1)
    grad_bias_table = small[3 * each : 3 * each + heads, :buckets].T
    attn_parts = hold(attn_parts, small)
    while attn_parts[0].bits:
        attn_parts = exchange_joined(attn_parts, to_send_joined(attn_parts, -2), -2, n)

    def both(own):
        got = swap_tower(own)
        first = jnp.where(tower == 0, own, got).astype(f32)
        second = jnp.where(tower == 0, got, own).astype(f32)
        return first, second

    grad_w_down = jnp.concatenate(both(down_own), axis=1).T
    gate_t, up_t = both(wide_own)
    attn_t = jnp.concatenate(both(finish(attn_parts, -2)), axis=1)
    return (
        output.reshape(tokens.shape),
        scores,
        grad_tokens.reshape(tokens.shape),
        attn_t[:narrow].T,
        attn_t[narrow : 2 * narrow].T,
        attn_t[2 * narrow : 3 * narrow].T,
        attn_t[3 * narrow :].T,
        gate_t.T,
        up_t.T,
        grad_w_down,
        gains[0],
        gains[1],
        gains[2],
        grad_bias_table,
    )


def solution(mesh):
    row = P("tower", "batch", None, None)
    in_specs = (row, P("tower", "batch", None)) + (P(),) * 11 + (row, P("batch", None))
    out_specs = (row, P("batch", None), row) + (P(None, "batch"),) * 7 + (P("batch"),) * 3 + (P(),)
    return jax.shard_map(
        functools.partial(body, mesh.shape["batch"]),
        mesh=mesh,
        in_specs=in_specs,
        out_specs=out_specs,
        check_vma=False,
    )
```
